128 devices in a mesh: dp: 32 (over y, x, core), mp: 4 (over z).
Axes of the slice: x: 4, y: 4, z: 4, core: 2. Of those that a mesh axis runs over, the one named last changes fastest.
Arguments:
- tokens: bfloat16 [8192, 4096], P('dp', 'mp'), may hold values from -6 to 6
- cotangent: bfloat16 [8192, 4096], P('dp', 'mp'), may hold values from -6 to 6
- database: bfloat16 [48, 64, 4096], P('mp'), may hold values from -6 to 6
- neighbour_ids: int32 [32, 4, 2], P('dp'), may hold values from 0 to 47, as said below
- valid_spans: int32 [32], P('dp'), may hold values from 1 to 4
- w_cq: bfloat16 [4096, 2048], P(None, 'mp'), may hold values from -0.09375 to 0.09375
- w_ck: bfloat16 [4096, 2048], P(None, 'mp'), may hold values from -0.09375 to 0.09375
- w_cv: bfloat16 [4096, 2048], P(None, 'mp'), may hold values from -0.09375 to 0.09375
- w_co: bfloat16 [2048, 4096], P('mp'), may hold values from -0.125 to 0.125
- w_eq: bfloat16 [4096, 2048], P(None, 'mp'), may hold values from -0.09375 to 0.09375
- w_ek: bfloat16 [4096, 2048], P(None, 'mp'), may hold values from -0.09375 to 0.09375
- w_ev: bfloat16 [4096, 2048], P(None, 'mp'), may hold values from -0.09375 to 0.09375
- w_eo: bfloat16 [2048, 4096], P('mp'), may hold values from -0.125 to 0.125
Outputs:
- output: bfloat16 [8192, 4096], P('dp', 'mp')
- d_input: bfloat16 [8192, 4096], P('dp', 'mp')
- d_database: float32 [48, 64, 4096], P('mp', None, 'dp')
- d_wco: float32 [2048, 4096], P('mp', 'dp')
The draws below stay inside these ranges and needn't reach their ends.
Inputs may be any that keep to these rules, and one draw needn't show every extreme that they name: `neighbour_ids`: the 8 neighbours of each aligned block of 1 sequence name at most 4 rows of any one database shard (rows r with the same r // 12), and exactly 4 of some shard.
All inputs are finite; a program needn't handle non-finite values.
Results may differ from the reference program's by a relative error of at most 0.035.
Values may be sent and summed in bfloat16 or wider, within the bound.
No kernel may reach another device: no remote copies, remote signals or barrier semaphores. Data moves between devices by JAX's collectives and lax.ppermute only.
A program may use at most 192 MiB of HBM per device.

```python
import math
import jax
import jax.numpy as jnp
from jax import lax

D = 4096
HEAD_DIM = 128
HEADS = 16
SPAN = 64
SPANS_SEQ = 4
K_NB = 2
NB_LEN = 64
SEQS_DEV = 1
CAP = 4
DB_DEV = 12
DB_ROWS = 48
SEQS = 32
TOKENS = 8192
N_DP = 32
N_MP = 4


def rough_field(key, shape):
    base = jnp.clip(jax.random.normal(key, shape, jnp.float32), -6.0, 6.0)
    return base


def draw_tokens(key, part):
    key = jax.random.fold_in(key, 3)
    return rough_field(key, (TOKENS, D)).astype(jnp.bfloat16)


def draw_database(key, part):
    key = jax.random.fold_in(key, 5)
    return rough_field(key, (DB_ROWS, NB_LEN, D)).astype(jnp.bfloat16)


def draw_neighbour_ids(key, part):
    key = jax.random.fold_in(key, 7)
    per_device = SEQS_DEV * SPANS_SEQ * K_NB
    entry_total = N_MP * CAP

    def one_device(device_key):
        perm_key, shuffle_key, row_key = jax.random.split(device_key, 3)
        entries = jax.random.permutation(perm_key, entry_total)
        owners = entries // CAP
        leading = owners[0]
        ordering = jnp.argsort(jnp.where(owners == leading, 0, 1), stable=True)
        picked = owners[ordering][:per_device]
        shuffled = jax.random.permutation(shuffle_key, picked)
        row_pick = jax.random.randint(row_key, (per_device,), 0, DB_DEV)
        return shuffled * DB_DEV + row_pick
    device_keys = jax.random.split(key, N_DP)
    chosen = jax.vmap(one_device)(device_keys)
    return chosen.reshape(SEQS, SPANS_SEQ, K_NB).astype(jnp.int32)


def draw_valid_spans(key, part):
    key = jax.random.fold_in(key, 11)
    counts_drawn = jax.random.randint(key, (SEQS,), 1, SPANS_SEQ + 1)
    return counts_drawn.at[0].set(SPANS_SEQ).astype(jnp.int32)


def raised(values, key, source, target, parts, factor):
    owner, partner = [(jnp.arange(values.shape[position]) // (values.shape[position] // parts)).reshape([-1 if axis == position else 1 for axis in range(values.ndim)]) for position in (source, target)]
    chosen = jax.random.permutation(key, parts)[partner]
    strong = (owner == chosen) | (owner == (partner + parts // 2) % parts)
    return jnp.where(strong, factor * values, values)


def block_levels(rng, dims, pieces, low, top_value):
    loudness, own = 1.0, jax.random.fold_in(rng, 6)
    for dim, shards_of in pieces:
        steps = jnp.exp(jax.random.uniform(jax.random.fold_in(own, dim), (shards_of,), jnp.float32, low / len(pieces), top_value / len(pieces)))
        loudness = loudness * jnp.repeat(steps, dims[dim] // shards_of).reshape([-1 if axis == dim else 1 for axis in range(len(dims))])
    return loudness


def normal_values(key, dims, deviation, limit, cuts=(), held_as=jnp.bfloat16):
    values = jax.random.normal(key, dims, jnp.float32) * deviation
    if len(cuts) > 0:
        values = block_levels(key, dims, cuts, -0.22, 0.18) * values
    return jnp.clip(values, min=-limit, max=limit).astype(held_as)


def bell_draw_with(own_key, dims, scale, bound, shards, heavy, held_as=jnp.bfloat16):
    result = scale * jax.random.normal(own_key, dims, jnp.float32)
    if shards:
        result = result * block_levels(own_key, dims, shards, -0.22, 0.18)
    return jnp.clip(raised(result, jax.random.fold_in(own_key, 3), *heavy), -bound, bound).astype(held_as)


def setup_inputs(seed: int = 0) -> dict:
    key_list = jax.random.split(jax.random.key(seed), 14)
    return {
        "tokens": draw_tokens(jax.random.fold_in(key_list[13], 71), 0),
        "cotangent": bell_draw_with(key_list[1], (TOKENS, D), 1.0, 6.0, ((0, 32), (1, 4)), (0, 1, 32, 2.75)),
        "database": draw_database(jax.random.fold_in(key_list[13], 71), 0),
        "neighbour_ids": draw_neighbour_ids(jax.random.fold_in(key_list[13], 71), 0),
        "valid_spans": draw_valid_spans(jax.random.fold_in(key_list[13], 71), 0),
        "w_cq": normal_values(key_list[5], (D, HEADS * HEAD_DIM), D ** -0.5, 0.09375, ((1, 4),)),
        "w_ck": normal_values(key_list[6], (D, HEADS * HEAD_DIM), D ** -0.5, 0.09375, ((1, 4),)),
        "w_cv": normal_values(key_list[7], (D, HEADS * HEAD_DIM), D ** -0.5, 0.09375, ((1, 4),)),
        "w_co": normal_values(key_list[8], (HEADS * HEAD_DIM, D), (HEADS * HEAD_DIM) ** -0.5, 0.125, ((0, 4),)),
        "w_eq": normal_values(key_list[9], (D, HEADS * HEAD_DIM), D ** -0.5, 0.09375, ((1, 4),)),
        "w_ek": normal_values(key_list[10], (D, HEADS * HEAD_DIM), D ** -0.5, 0.09375, ((1, 4),)),
        "w_ev": normal_values(key_list[11], (D, HEADS * HEAD_DIM), D ** -0.5, 0.09375, ((1, 4),)),
        "w_eo": normal_values(key_list[12], (HEADS * HEAD_DIM, D), (HEADS * HEAD_DIM) ** -0.5, 0.125, ((0, 4),)),
    }


def project(operand, matrix):
    return jnp.dot(operand, matrix, preferred_element_type=jnp.float32)

def attend(queries, key_rows, value_rows):
    inv_scale = 1.0 / math.sqrt(queries.shape[-1])
    scores = jnp.einsum('bqhe,bkhe->bhqk', queries.astype(jnp.float32), key_rows.astype(jnp.float32)) * inv_scale
    soft_probs = jax.nn.softmax(scores, axis=-1)
    weights = soft_probs.astype(jnp.bfloat16)
    mixed_out = jnp.einsum('bhqk,bkhe->bqhe', weights.astype(jnp.float32), value_rows.astype(jnp.float32)).astype(jnp.bfloat16)
    return (mixed_out, soft_probs, weights)

def attend_back(queries, key_rows, value_rows, soft_probs, weights, upstream):
    inv_scale = 1.0 / math.sqrt(queries.shape[-1])
    d_weights = jnp.einsum('bqhe,bkhe->bhqk', upstream.astype(jnp.float32), value_rows.astype(jnp.float32))
    row_inner = lax.optimization_barrier(jnp.sum(d_weights * soft_probs, axis=-1, keepdims=True))
    d_scores = (soft_probs * (d_weights - row_inner)).astype(jnp.bfloat16)
    d_query = (jnp.einsum('bhqk,bkhe->bqhe', d_scores.astype(jnp.float32), key_rows.astype(jnp.float32)) * inv_scale).astype(jnp.bfloat16)
    d_keys = (jnp.einsum('bhqk,bqhe->bkhe', d_scores.astype(jnp.float32), queries.astype(jnp.float32)) * inv_scale).astype(jnp.bfloat16)
    d_values = jnp.einsum('bhqk,bqhe->bkhe', weights.astype(jnp.float32), upstream.astype(jnp.float32)).astype(jnp.bfloat16)
    return (d_query, d_keys, d_values)

def grouped(term_pairs):
    group_width = term_pairs[0][0].shape[1] // N_MP
    running = jnp.zeros((term_pairs[0][0].shape[0], term_pairs[0][1].shape[1]), jnp.float32)
    for group_index in range(N_MP):
        begin = group_index * group_width
        partial_sum = jnp.zeros_like(running)
        for operand, matrix in term_pairs:
            partial_sum = partial_sum + project(operand[:, begin:begin + group_width], matrix[begin:begin + group_width])
        rounded = lax.optimization_barrier(partial_sum.astype(jnp.bfloat16))
        running = running + rounded.astype(jnp.float32)
    return running

def reference(tokens, cotangent, database, neighbour_ids, valid_spans, w_cq, w_ck, w_cv, w_co, w_eq, w_ek, w_ev, w_eo):
    span_total = SEQS * SPANS_SEQ
    per_span = K_NB * NB_LEN
    full_width = HEADS * HEAD_DIM

    def split_heads(values_in, length):
        return values_in.reshape(span_total, length, HEADS, HEAD_DIM)
    flat_ids = neighbour_ids.reshape(-1).astype(jnp.int32)
    neighbours = database[flat_ids].reshape(-1, D)
    span_q = project(tokens, w_cq).astype(jnp.bfloat16)
    enc_k = project(tokens, w_ek).astype(jnp.bfloat16)
    enc_v = project(tokens, w_ev).astype(jnp.bfloat16)
    enc_q = project(neighbours, w_eq).astype(jnp.bfloat16)
    enc_qh = split_heads(enc_q, per_span)
    enc_kh = split_heads(enc_k, SPAN)
    enc_vh = split_heads(enc_v, SPAN)
    enc_mixed, enc_probs, enc_weights = attend(enc_qh, enc_kh, enc_vh)
    enc_flat = enc_mixed.reshape(-1, full_width)
    encoded = (neighbours.astype(jnp.float32) + grouped([(enc_flat, w_eo)])).astype(jnp.bfloat16)
    cross_k = project(encoded, w_ck).astype(jnp.bfloat16)
    cross_v = project(encoded, w_cv).astype(jnp.bfloat16)
    cross_qh = split_heads(span_q, SPAN)
    cross_kh = split_heads(cross_k, per_span)
    cross_vh = split_heads(cross_v, per_span)
    cross_mixed, cross_probs, cross_weights = attend(cross_qh, cross_kh, cross_vh)
    cross_flat = cross_mixed.reshape(-1, full_width)
    live = jnp.arange(SPANS_SEQ)[None, :] < valid_spans[:, None]
    live_tok = jnp.repeat(live.reshape(-1), SPAN)[:, None]
    output = (tokens.astype(jnp.float32) + jnp.where(live_tok, grouped([(cross_flat, w_co)]), 0.0)).astype(jnp.bfloat16)
    gated = jnp.where(live_tok, cotangent, jnp.zeros_like(cotangent))
    d_wco = project(cross_flat.T, gated)
    d_cross = project(gated, w_co.T).astype(jnp.bfloat16)
    d_cq, d_ck, d_cv = attend_back(cross_qh, cross_kh, cross_vh, cross_probs, cross_weights, split_heads(d_cross, SPAN))
    d_encoded = grouped([(d_ck.reshape(-1, full_width), w_ck.T), (d_cv.reshape(-1, full_width), w_cv.T)]).astype(jnp.bfloat16)
    d_enc_heads = project(d_encoded, w_eo.T).astype(jnp.bfloat16)
    d_eq, d_ek, d_ev = attend_back(enc_qh, enc_kh, enc_vh, enc_probs, enc_weights, split_heads(d_enc_heads, per_span))
    d_nbr = (d_encoded.astype(jnp.float32) + grouped([(d_eq.reshape(-1, full_width), w_eq.T)])).astype(jnp.bfloat16)
    d_database = jnp.zeros((DB_ROWS, NB_LEN * D), jnp.float32).at[flat_ids].add(d_nbr.reshape(-1, NB_LEN * D).astype(jnp.float32))
    d_database = d_database.reshape(DB_ROWS, NB_LEN, D)
    token_terms = grouped([(d_cq.reshape(-1, full_width), w_cq.T), (d_ek.reshape(-1, full_width), w_ek.T), (d_ev.reshape(-1, full_width), w_ev.T)])
    d_input = (cotangent.astype(jnp.float32) + token_terms).astype(jnp.bfloat16)
    return (output, d_input, d_database, d_wco)
```

```python
import functools
import math

import jax
import jax.numpy as jnp
from jax import lax
from jax.experimental import pallas as pl
from jax.experimental.pallas import tpu as pltpu
from jax.sharding import PartitionSpec as P

HEAD_DIM = 128
SPAN = 64
SPANS_SEQ = 4
K_NB = 2
INV_SCALE = 1.0 / math.sqrt(HEAD_DIM)
VMEM_LIMIT = 48 * 1024 * 1024


def dot(a, b):
    return jnp.dot(a, b, preferred_element_type=jnp.float32)


def dot_nt(a, b):
    return lax.dot_general(a, b, (((1,), (1,)), ((), ())), preferred_element_type=jnp.float32)


def dot_tn(a, b):
    return lax.dot_general(a, b, (((0,), (0,)), ((), ())), preferred_element_type=jnp.float32)


def to_right(x):
    n = lax.axis_size("mp")
    return lax.ppermute(x, "mp", [(i, (i + 1) % n) for i in range(n)])


def to_left(x):
    n = lax.axis_size("mp")
    return lax.ppermute(x, "mp", [(i, (i - 1) % n) for i in range(n)])


def ring_gather(x):
    half = x.shape[0] // 2
    prev = to_right(x)
    following = to_left(x)
    opp_a = to_right(prev[:half])
    opp_b = to_left(following[half:])
    return [x, following, jnp.concatenate([opp_a, opp_b], axis=0), prev]


def ring_scatter(blocks):
    own, following, opp, prev = blocks
    half = own.shape[0] // 2
    f32 = jnp.float32
    from_left = to_right(jnp.concatenate([opp[:half], following[half:]], axis=0))
    from_right = to_left(jnp.concatenate([prev[:half], opp[half:]], axis=0))
    pass_right = (following[:half].astype(f32) + from_left[:half].astype(f32)).astype(own.dtype)
    pass_left = (prev[half:].astype(f32) + from_right[half:].astype(f32)).astype(own.dtype)
    low = to_right(pass_right)
    high = to_left(pass_left)
    total_low = own[:half].astype(f32) + from_right[:half].astype(f32) + low.astype(f32)
    total_high = own[half:].astype(f32) + from_left[half:].astype(f32) + high.astype(f32)
    return jnp.concatenate([total_low, total_high], axis=0)


def order_matrix(rows, sources):
    per_span = rows // SPANS_SEQ
    chunk = per_span // sources
    out_row = lax.broadcasted_iota(jnp.int32, (rows, rows), 0)
    in_row = lax.broadcasted_iota(jnp.int32, (rows, rows), 1)
    span = out_row // per_span
    source = (out_row % per_span) // chunk
    place = source * (chunk * SPANS_SEQ) + span * chunk + out_row % chunk
    return jnp.where(in_row == place, 1.0, 0.0).astype(jnp.bfloat16)


def softmax_rows(scores):
    top = jnp.max(scores, axis=-1, keepdims=True)
    grown = jnp.exp(scores - top)
    return grown / jnp.sum(grown, axis=-1, keepdims=True)


def back_one(q, k, v, u, probs, weights):
    d_weights = dot_nt(u, v)
    inner = jnp.sum(d_weights * probs, axis=-1, keepdims=True)
    d_scores = (probs * (d_weights - inner)).astype(jnp.bfloat16)
    d_q = (dot(d_scores, k) * INV_SCALE).astype(jnp.bfloat16)
    d_k = (dot_tn(d_scores, q) * INV_SCALE).astype(jnp.bfloat16)
    d_v = dot_tn(weights, u).astype(jnp.bfloat16)
    return d_q, d_k, d_v


def tiles(q_rows, k_rows, heads):
    for span in range(SPANS_SEQ):
        for head in range(heads):
            cols = slice(head * HEAD_DIM, (head + 1) * HEAD_DIM)
            yield (
                slice(span * q_rows, (span + 1) * q_rows),
                slice(span * k_rows, (span + 1) * k_rows),
                cols,
            )


def enc_forward_kernel(sources, q_ref, k_ref, v_ref, out_ref, q_s, o_s):
    rows, width = q_ref.shape
    order = order_matrix(rows, sources)
    q_s[...] = dot(order, q_ref[...]).astype(jnp.bfloat16)
    for qs, ks, cols in tiles(rows // SPANS_SEQ, SPAN, width // HEAD_DIM):
        probs = softmax_rows(dot_nt(q_s[qs, cols], k_ref[ks, cols]) * INV_SCALE)
        o_s[qs, cols] = dot(probs.astype(jnp.bfloat16), v_ref[ks, cols]).astype(jnp.bfloat16)
    out_ref[...] = dot_tn(order, o_s[...]).astype(jnp.bfloat16)


def enc_backward_kernel(
    sources, q_ref, k_ref, v_ref, u_ref, dq_ref, dk_ref, dv_ref, q_s, u_s, dq_s
):
    rows, width = q_ref.shape
    order = order_matrix(rows, sources)
    q_s[...] = dot(order, q_ref[...]).astype(jnp.bfloat16)
    u_s[...] = dot(order, u_ref[...]).astype(jnp.bfloat16)
    for qs, ks, cols in tiles(rows // SPANS_SEQ, SPAN, width // HEAD_DIM):
        q, k, v, u = q_s[qs, cols], k_ref[ks, cols], v_ref[ks, cols], u_s[qs, cols]
        probs = softmax_rows(dot_nt(q, k) * INV_SCALE)
        d_q, d_k, d_v = back_one(q, k, v, u, probs, probs.astype(jnp.bfloat16))
        dq_s[qs, cols] = d_q
        dk_ref[ks, cols] = d_k
        dv_ref[ks, cols] = d_v
    dq_ref[...] = dot_tn(order, dq_s[...]).astype(jnp.bfloat16)


def cross_kernel(
    sources, q_ref, k_ref, v_ref, u_ref, o_ref, dq_ref, dk_ref, dv_ref, k_s, v_s, dk_s, dv_s
):
    rows, width = k_ref.shape
    order = order_matrix(rows, sources)
    k_s[...] = dot(order, k_ref[...]).astype(jnp.bfloat16)
    v_s[...] = dot(order, v_ref[...]).astype(jnp.bfloat16)
    for qs, ks, cols in tiles(SPAN, rows // SPANS_SEQ, width // HEAD_DIM):
        q, k, v, u = q_ref[qs, cols], k_s[ks, cols], v_s[ks, cols], u_ref[qs, cols]
        probs = softmax_rows(dot_nt(q, k) * INV_SCALE)
        weights = probs.astype(jnp.bfloat16)
        o_ref[qs, cols] = dot(weights, v).astype(jnp.bfloat16)
        d_q, d_k, d_v = back_one(q, k, v, u, probs, weights)
        dq_ref[qs, cols] = d_q
        dk_s[ks, cols] = d_k
        dv_s[ks, cols] = d_v
    dk_ref[...] = dot_tn(order, dk_s[...]).astype(jnp.bfloat16)
    dv_ref[...] = dot_tn(order, dv_s[...]).astype(jnp.bfloat16)


def attention_call(body, sources, operands, outs, scratch, flops):
    vmem = pl.BlockSpec(memory_space=pltpu.VMEM)
    moved = 2 * (sum(math.prod(x.shape) for x in operands) + sum(math.prod(s) for s in outs))
    return pl.pallas_call(
        functools.partial(body, sources),
        out_shape=[jax.ShapeDtypeStruct(s, jnp.bfloat16) for s in outs],
        in_specs=[vmem] * len(operands),
        out_specs=[vmem] * len(outs),
        scratch_shapes=[pltpu.VMEM(s, jnp.bfloat16) for s in scratch],
        compiler_params=pltpu.CompilerParams(vmem_limit_bytes=VMEM_LIMIT),
        cost_estimate=pl.CostEstimate(flops=flops, bytes_accessed=moved, transcendentals=0),
    )(*operands)


def feature_kernel(count, rows_of_weight, z_ref, *refs):
    out_ref = refs[-1]
    total = None
    for d_ref, w_ref in zip(refs[:count], refs[count : 2 * count]):
        part = dot_nt(d_ref[...], w_ref[...]) if rows_of_weight else dot(d_ref[...], w_ref[...])
        total = part if total is None else total + part
    out_ref[0] = total.astype(jnp.bfloat16)


def feature_products(operands, weights, z, rows_of_weight):
    rows, depth = operands[0].shape
    model = weights[0].shape[0 if rows_of_weight else 1]
    planes = lax.axis_size("mp")
    step = 512
    per = model // planes // step

    def place(j, z_ref):
        return ((z_ref[0] + j // per) % planes) * per + j % per

    if rows_of_weight:
        w_spec = pl.BlockSpec((step, depth), lambda j, z_ref: (place(j, z_ref), 0))
    else:
        w_spec = pl.BlockSpec((depth, step), lambda j, z_ref: (0, place(j, z_ref)))
    n = len(operands)
    return pl.pallas_call(
        functools.partial(feature_kernel, n, rows_of_weight),
        out_shape=jax.ShapeDtypeStruct((planes, rows, model // planes), jnp.bfloat16),
        grid_spec=pltpu.PrefetchScalarGridSpec(
            num_scalar_prefetch=1,
            grid=(planes * per,),
            in_specs=[pl.BlockSpec((rows, depth), lambda j, z_ref: (0, 0))] * n + [w_spec] * n,
            out_specs=pl.BlockSpec((1, rows, step), lambda j, z_ref: (j // per, 0, j % per)),
        ),
        compiler_params=pltpu.CompilerParams(vmem_limit_bytes=VMEM_LIMIT),
        cost_estimate=pl.CostEstimate(
            flops=2 * n * rows * depth * model,
            bytes_accessed=2 * n * (rows * depth + depth * model) + 2 * rows * model,
            transcendentals=0,
        ),
    )(z.reshape(1), *operands, *weights)


def on_device(
    tokens,
    cotangent,
    database,
    neighbour_ids,
    valid_spans,
    w_cq,
    w_ck,
    w_cv,
    w_co,
    w_eq,
    w_ek,
    w_ev,
    w_eo,
):
    bf16, f32 = jnp.bfloat16, jnp.float32
    width = w_cq.shape[1]
    heads = width // HEAD_DIM
    tok_rows, feat_here = tokens.shape
    model = w_cq.shape[0]
    db_here, nbr_len, _ = database.shape
    planes = lax.axis_size("mp")
    sources = lax.axis_size("dp")
    z = lax.axis_index("mp")
    i = lax.axis_index("dp")
    nbr_count = neighbour_ids.size
    part = nbr_len // sources
    db_rows = db_here * part
    eo_rows = width // sources
    nbr_total = nbr_count * nbr_len

    db_own = lax.dynamic_slice_in_dim(database, i * part, part, 1).reshape(db_rows, model)
    eo_own = lax.dynamic_slice_in_dim(w_eo, i * eo_rows, eo_rows, 0)
    gathered = ring_gather(jnp.concatenate([db_own, eo_own], axis=0))
    mixed_rows = jnp.concatenate(
        [g[:db_rows] for g in gathered] + [g[db_rows:] for g in gathered], axis=0
    )
    ids = lax.all_gather(neighbour_ids.reshape(-1), "dp", axis=0, tiled=True)

    held_rows = planes * db_rows
    row_k = dot(mixed_rows, w_ck).astype(bf16)
    row_v = dot(mixed_rows, w_cv).astype(bf16)
    row_q = dot(mixed_rows[:held_rows], w_eq).astype(bf16)
    share = jnp.concatenate([row_k[held_rows:], row_v[held_rows:]], axis=1)
    composite = lax.all_gather(
        share.reshape(planes, eo_rows, 2 * width), "dp", axis=1, tiled=True
    )

    held = lax.broadcasted_iota(jnp.int32, (1, held_rows), 1)
    held_id = ((z + held // db_rows) % planes) * db_here + (held % db_rows) // part
    held_tok = held % part
    asked = jnp.repeat(ids, part)[:, None]
    asked_tok = lax.broadcasted_iota(jnp.int32, (nbr_total, 1), 0) % part
    pick = ((asked == held_id) & (asked_tok == held_tok)).astype(bf16)

    def spread(x):
        return lax.all_to_all(x, "dp", split_axis=0, concat_axis=0, tiled=True)

    enc_q = spread(dot(pick, row_q).astype(bf16))
    nbr_kv = spread(
        dot(pick, jnp.concatenate([row_k[:held_rows], row_v[:held_rows]], axis=1)).astype(bf16)
    )

    tok_full = lax.all_gather(tokens, "mp", axis=1, tiled=True)
    enc_k = dot(tok_full, w_ek).astype(bf16)
    enc_v = dot(tok_full, w_ev).astype(bf16)
    span_q = dot(tok_full, w_cq).astype(bf16)

    live = jnp.arange(SPANS_SEQ)[None, :] < valid_spans[:, None]
    live_tok = jnp.repeat(live.reshape(-1), SPAN)[:, None]
    cot_full = jnp.zeros((tok_rows, model), bf16)
    for b, block in enumerate(ring_gather(cotangent)):
        cot_full = lax.dynamic_update_slice_in_dim(
            cot_full, block, ((z + b) % planes) * feat_here, 1
        )
    gated = jnp.where(live_tok, cot_full, jnp.zeros_like(cot_full))
    d_cross = dot_nt(gated, w_co).astype(bf16)

    attn_flops = 2 * nbr_total * SPAN * width
    sort_flops = 2 * nbr_total * nbr_total * width
    wide = (nbr_total, width)
    narrow = (tok_rows, width)
    (enc_mixed,) = attention_call(
        enc_forward_kernel,
        sources,
        (enc_q, enc_k, enc_v),
        [wide],
        [wide, wide],
        2 * attn_flops + 2 * sort_flops,
    )
    enc_all = jnp.concatenate(ring_gather(enc_mixed), axis=1)
    kv = (
        dot(enc_all, composite.reshape(planes * width, 2 * width)) + nbr_kv.astype(f32)
    ).astype(bf16)
    cross_k, cross_v = kv[:, :width], kv[:, width:]
    cross_mixed, d_cq, d_ck, d_cv = attention_call(
        cross_kernel,
        sources,
        (span_q, cross_k, cross_v, d_cross),
        [narrow, narrow, wide, wide],
        [wide] * 4,
        6 * attn_flops + 4 * sort_flops,
    )

    d_wco = lax.psum_scatter(
        dot_tn(cross_mixed, gated).astype(bf16), "dp", scatter_dimension=1, tiled=True
    ).astype(f32)
    out_terms = feature_products([cross_mixed], [w_co], z, False)
    out_part = ring_scatter([out_terms[b] for b in range(planes)])
    output = (tokens.astype(f32) + jnp.where(live_tok, out_part, 0.0)).astype(bf16)

    d_kv = jnp.concatenate([d_ck, d_cv], axis=1)
    d_enc = ring_scatter([dot_nt(d_kv, composite[b]).astype(bf16) for b in range(planes)])
    d_kv_back = spread(d_kv)
    d_eq, d_ek, d_ev = attention_call(
        enc_backward_kernel,
        sources,
        (enc_q, enc_k, enc_v, d_enc.astype(bf16)),
        [wide, narrow, narrow],
        [wide] * 3,
        5 * attn_flops + 3 * sort_flops,
    )
    d_q_back = spread(d_eq)
    tok_terms = feature_products([d_cq, d_ek, d_ev], [w_cq, w_ek, w_ev], z, True)
    tok_part = ring_scatter([tok_terms[b] for b in range(planes)])
    d_input = (cotangent.astype(f32) + tok_part).astype(bf16)

    sum_kv = dot_tn(pick, d_kv_back).astype(bf16)
    sum_q = dot_tn(pick, d_q_back).astype(bf16)
    db_terms = (
        dot_nt(sum_kv[:, :width], w_ck) + dot_nt(sum_kv[:, width:], w_cv) + dot_nt(sum_q, w_eq)
    ).astype(bf16)
    db_terms = db_terms.reshape(planes, db_rows, sources, model // sources)
    db_terms = jnp.stack(
        [
            lax.dynamic_index_in_dim(db_terms, (p - z) % planes, 0, keepdims=False)
            for p in range(planes)
        ]
    )
    db_terms = db_terms.transpose(2, 0, 1, 3).reshape(sources * planes, db_rows, model // sources)
    arrived = lax.all_to_all(db_terms, ("dp", "mp"), split_axis=0, concat_axis=0, tiled=True)
    arrived = arrived.reshape(sources, planes, db_here, part, model // sources)
    d_database = (
        jnp.sum(arrived.astype(f32), axis=1)
        .transpose(1, 0, 2, 3)
        .reshape(db_here, nbr_len, model // sources)
    )
    return (output, d_input, d_database, d_wco)


def solution(mesh):
    placed = (
        P("dp", "mp"),
        P("dp", "mp"),
        P("mp", None, None),
        P("dp", None, None),
        P("dp"),
        P(None, "mp"),
        P(None, "mp"),
        P(None, "mp"),
        P("mp", None),
        P(None, "mp"),
        P(None, "mp"),
        P(None, "mp"),
        P("mp", None),
    )
    return jax.shard_map(
        on_device,
        mesh=mesh,
        in_specs=placed,
        out_specs=(P("dp", "mp"), P("dp", "mp"), P("mp", None, "dp"), P("mp", "dp")),
        check_vma=False,
    )
```

```python
import functools
import math

import jax
import jax.numpy as jnp
from jax import lax
from jax.experimental import pallas as pl
from jax.experimental.pallas import tpu as pltpu
from jax.sharding import PartitionSpec as P

HEAD_DIM = 128
SPAN = 64
SPANS_SEQ = 4
K_NB = 2
INV_SCALE = 1.0 / math.sqrt(HEAD_DIM)
VMEM_LIMIT = 48 * 1024 * 1024


def dot(a, b):
    return jnp.dot(a, b, preferred_element_type=jnp.float32)


def dot_nt(a, b):
    return lax.dot_general(a, b, (((1,), (1,)), ((), ())), preferred_element_type=jnp.float32)


def dot_tn(a, b):
    return lax.dot_general(a, b, (((0,), (0,)), ((), ())), preferred_element_type=jnp.float32)


def to_right(x):
    n = lax.axis_size("mp")
    return lax.ppermute(x, "mp", [(i, (i + 1) % n) for i in range(n)])


def to_left(x):
    n = lax.axis_size("mp")
    return lax.ppermute(x, "mp", [(i, (i - 1) % n) for i in range(n)])


def ring_first(x):
    return to_left(x), to_right(x)


def ring_second(following, prev):
    half = prev.shape[0] // 2
    return to_right(prev[:half]), to_left(following[half:])


def ring_gather(x):
    following, prev = ring_first(x)
    opp_a, opp_b = ring_second(following, prev)
    return [x, following, jnp.concatenate([opp_a, opp_b], axis=0), prev]


def scatter_sends(blocks):
    own, following, opp, prev = blocks
    half = own.shape[0] // 2
    return (
        jnp.concatenate([opp[:half], following[half:]], axis=0),
        jnp.concatenate([prev[:half], opp[half:]], axis=0),
    )


def scatter_first(blocks):
    rightward, leftward = scatter_sends(blocks)
    return to_right(rightward), to_left(leftward)


def scatter_second(blocks, from_left, from_right):
    own, following, opp, prev = blocks
    half = own.shape[0] // 2
    f32 = jnp.float32
    pass_right = (following[:half].astype(f32) + from_left[:half].astype(f32)).astype(own.dtype)
    pass_left = (prev[half:].astype(f32) + from_right[half:].astype(f32)).astype(own.dtype)
    return own, from_left, from_right, to_right(pass_right), to_left(pass_left)


def scatter_sum(own, from_left, from_right, low, high):
    half = own.shape[0] // 2
    f32 = jnp.float32
    total_low = own[:half].astype(f32) + from_right[:half].astype(f32) + low[...].astype(f32)
    total_high = own[half:].astype(f32) + from_left[half:].astype(f32) + high[...].astype(f32)
    return jnp.concatenate([total_low, total_high], axis=0)


def place_blocks(z_ref, blocks, out_ref):
    planes = lax.axis_size("mp")
    wide = blocks[0].shape[1]
    half = blocks[2].shape[0]

    def at(b):
        return pl.ds(pl.multiple_of(((z_ref[0] + b) % planes) * wide, wide), wide)

    out_ref[:, at(0)] = blocks[0][...]
    out_ref[:, at(1)] = blocks[1][...]
    out_ref[:half, at(2)] = blocks[2][...]
    out_ref[half:, at(2)] = blocks[3][...]
    out_ref[:, at(3)] = blocks[4][...]


def tokens_kernel(z_ref, *refs):
    place_blocks(z_ref, refs[:5], refs[5])


def cotangent_kernel(z_ref, live_ref, *refs):
    live = live_ref[...] > 0
    kept = [jnp.where(live[: r.shape[0]], r[...], jnp.zeros_like(r)) for r in refs[:3]]
    kept.append(jnp.where(live[refs[2].shape[0] :], refs[3][...], jnp.zeros_like(refs[3])))
    kept.append(jnp.where(live, refs[4][...], jnp.zeros_like(refs[4])))
    place_blocks(z_ref, kept, refs[5])


def assemble(body, scalars, operands, outs):
    vmem = pl.BlockSpec(memory_space=pltpu.VMEM)
    smem = pl.BlockSpec(memory_space=pltpu.SMEM)
    return pl.pallas_call(
        body,
        out_shape=[jax.ShapeDtypeStruct(s, jnp.bfloat16) for s in outs],
        in_specs=[smem] * len(scalars) + [vmem] * len(operands),
        out_specs=[vmem] * len(outs),
        compiler_params=pltpu.CompilerParams(vmem_limit_bytes=VMEM_LIMIT),
        cost_estimate=pl.CostEstimate(
            flops=0, bytes_accessed=4 * sum(math.prod(s) for s in outs), transcendentals=0
        ),
    )(*[x.reshape(1) for x in scalars], *operands)


def order_matrix(rows, sources, inverse):
    per_span = rows // SPANS_SEQ
    chunk = per_span // sources
    block = chunk * SPANS_SEQ
    row = lax.broadcasted_iota(jnp.int32, (rows, 1), 0)
    column = lax.broadcasted_iota(jnp.int32, (rows, rows), 1)
    if inverse:
        place = ((row % block) // chunk) * per_span + (row // block) * chunk + row % chunk
    else:
        place = ((row % per_span) // chunk) * block + (row // per_span) * chunk + row % chunk
    return jnp.where(column == place, 1.0, 0.0).astype(jnp.bfloat16)


def reorder(order, rows):
    return dot(order, rows).astype(jnp.bfloat16)


def softmax_rows(scores):
    top = jnp.max(scores, axis=-1, keepdims=True)
    grown = jnp.exp(scores - top)
    return grown * (1.0 / jnp.sum(grown, axis=-1, keepdims=True))


def tiles(q_rows, k_rows, heads):
    return [
        (
            slice(span * q_rows, (span + 1) * q_rows),
            slice(span * k_rows, (span + 1) * k_rows),
            slice(head * HEAD_DIM, (head + 1) * HEAD_DIM),
        )
        for span in range(SPANS_SEQ)
        for head in range(heads)
    ]


def all_probs(places, q_ref, k_ref):
    scores = [dot_nt(q_ref[q, c], k_ref[k, c]) for q, k, c in places]
    return softmax_rows(jnp.concatenate(scores, axis=0) * INV_SCALE)


def all_backward(places, probs, weights, q_ref, k_ref, v_ref, u_ref, dq_ref, dk_ref, dv_ref):
    d_weights = jnp.concatenate([dot_nt(u_ref[q, c], v_ref[k, c]) for q, k, c in places], axis=0)
    inner = jnp.sum(d_weights * probs, axis=-1, keepdims=True)
    d_scores = (probs * (d_weights - inner)).astype(jnp.bfloat16)
    rows = probs.shape[0] // len(places)
    for n, (q, k, c) in enumerate(places):
        d_s = d_scores[n * rows : (n + 1) * rows]
        dq_ref[q, c] = (dot(d_s, k_ref[k, c]) * INV_SCALE).astype(jnp.bfloat16)
    for n, (q, k, c) in enumerate(places):
        d_s, w = d_scores[n * rows : (n + 1) * rows], weights[n * rows : (n + 1) * rows]
        dk_ref[k, c] = (dot_tn(d_s, q_ref[q, c]) * INV_SCALE).astype(jnp.bfloat16)
        dv_ref[k, c] = dot_tn(w, u_ref[q, c]).astype(jnp.bfloat16)


def mix(places, weights, v_ref, out_ref):
    rows = weights.shape[0] // len(places)
    for n, (q, k, c) in enumerate(places):
        out_ref[q, c] = dot(weights[n * rows : (n + 1) * rows], v_ref[k, c]).astype(jnp.bfloat16)


def enc_forward_kernel(sources, n_ref, k_ref, v_ref, out_ref, q_s, o_s):
    rows, width = out_ref.shape
    q_s[...] = reorder(order_matrix(rows, sources, False), n_ref[:, :width])
    places = tiles(rows // SPANS_SEQ, SPAN, width // HEAD_DIM)
    mix(places, all_probs(places, q_s, k_ref).astype(jnp.bfloat16), v_ref, o_s)
    out_ref[...] = reorder(order_matrix(rows, sources, True), o_s[...])


def enc_backward_kernel(sources, n_ref, k_ref, v_ref, *refs):
    terms, (dq_ref, dk_ref, dv_ref, q_s, u_s, dq_s) = refs[:5], refs[5:]
    rows, width = dq_ref.shape
    order = order_matrix(rows, sources, False)
    q_s[...] = reorder(order, n_ref[:, :width])
    u_s[...] = reorder(order, scatter_sum(*terms).astype(jnp.bfloat16))
    places = tiles(rows // SPANS_SEQ, SPAN, width // HEAD_DIM)
    probs = all_probs(places, q_s, k_ref)
    weights = probs.astype(jnp.bfloat16)
    all_backward(places, probs, weights, q_s, k_ref, v_ref, u_s, dq_s, dk_ref, dv_ref)
    dq_ref[...] = reorder(order_matrix(rows, sources, True), dq_s[...])


def cross_kernel(sources, q_ref, kv_ref, u_ref, o_ref, dq_ref, dkv_ref, k_s, v_s, dk_s, dv_s):
    rows, both = kv_ref.shape
    width = both // 2
    order = order_matrix(rows, sources, False)
    k_s[...] = reorder(order, kv_ref[:, :width])
    v_s[...] = reorder(order, kv_ref[:, width:])
    places = tiles(SPAN, rows // SPANS_SEQ, width // HEAD_DIM)
    probs = all_probs(places, q_ref, k_s)
    weights = probs.astype(jnp.bfloat16)
    mix(places, weights, v_s, o_ref)
    all_backward(places, probs, weights, q_ref, k_s, v_s, u_ref, dq_ref, dk_s, dv_s)
    back = order_matrix(rows, sources, True)
    dkv_ref[:, :width] = reorder(back, dk_s[...])
    dkv_ref[:, width:] = reorder(back, dv_s[...])


def attention_call(body, sources, operands, outs, scratch, flops):
    vmem = pl.BlockSpec(memory_space=pltpu.VMEM)
    moved = 2 * (sum(math.prod(x.shape) for x in operands) + sum(math.prod(s) for s in outs))
    return pl.pallas_call(
        functools.partial(body, sources),
        out_shape=[jax.ShapeDtypeStruct(s, jnp.bfloat16) for s in outs],
        in_specs=[vmem] * len(operands),
        out_specs=[vmem] * len(outs),
        scratch_shapes=[pltpu.VMEM(s, jnp.bfloat16) for s in scratch],
        compiler_params=pltpu.CompilerParams(vmem_limit_bytes=VMEM_LIMIT),
        cost_estimate=pl.CostEstimate(flops=flops, bytes_accessed=moved, transcendentals=0),
    )(*operands)


def on_device(
    tokens,
    cotangent,
    database,
    neighbour_ids,
    valid_spans,
    w_cq,
    w_ck,
    w_cv,
    w_co,
    w_eq,
    w_ek,
    w_ev,
    w_eo,
):
    bf16, f32 = jnp.bfloat16, jnp.float32
    width = w_cq.shape[1]
    heads = width // HEAD_DIM
    tok_rows, feat_here = tokens.shape
    model = w_cq.shape[0]
    db_here, nbr_len, _ = database.shape
    planes = lax.axis_size("mp")
    sources = lax.axis_size("dp")
    z = lax.axis_index("mp")
    i = lax.axis_index("dp")
    nbr_count = neighbour_ids.size
    part = nbr_len // sources
    db_rows = db_here * part
    eo_rows = width // sources
    nbr_total = nbr_count * nbr_len

    def spread(x):
        return lax.all_to_all(x, "dp", split_axis=0, concat_axis=0, tiled=True)

    db_own = lax.dynamic_slice_in_dim(database, i * part, part, 1).reshape(db_rows, model)
    eo_own = lax.dynamic_slice_in_dim(w_eo, i * eo_rows, eo_rows, 0)
    rows_own = jnp.concatenate([db_own, eo_own], axis=0)
    rows_following, rows_prev = ring_first(rows_own)
    rows_following, rows_prev, asked_here = lax.optimization_barrier(
        (rows_following, rows_prev, neighbour_ids.reshape(1, -1))
    )
    ids = spread(jnp.broadcast_to(asked_here, (sources, nbr_count))).reshape(-1)
    rows_opp = jnp.concatenate(ring_second(rows_following, rows_prev), axis=0)
    gathered = [rows_own, rows_following, rows_opp, rows_prev]
    mixed_rows = jnp.concatenate(
        [g[:db_rows] for g in gathered] + [g[db_rows:] for g in gathered], axis=0
    )
    mixed_rows, ids, tok_here = lax.optimization_barrier((mixed_rows, ids, tokens))
    tok_following, tok_prev = ring_first(tok_here)

    held_rows = planes * db_rows
    row_k = dot(mixed_rows, w_ck).astype(bf16)
    row_v = dot(mixed_rows, w_cv).astype(bf16)
    row_q = dot(mixed_rows[:held_rows], w_eq).astype(bf16)
    share = jnp.concatenate([row_k[held_rows:], row_v[held_rows:]], axis=1)
    composite = lax.all_gather(
        share.reshape(planes, eo_rows, 2 * width), "dp", axis=1, tiled=True
    )

    held = lax.broadcasted_iota(jnp.int32, (1, held_rows), 1)
    held_id = ((z + held // db_rows) % planes) * db_here + (held % db_rows) // part
    held_tok = held % part
    asked = jnp.repeat(ids, part)[:, None]
    asked_tok = lax.broadcasted_iota(jnp.int32, (nbr_total, 1), 0) % part
    pick = ((asked == held_id) & (asked_tok == held_tok)).astype(bf16)
    row_all = jnp.concatenate([row_q, row_k[:held_rows], row_v[:held_rows]], axis=1)
    nbr_all = spread(dot(pick, row_all).astype(bf16))

    tok_opp = ring_second(tok_following, tok_prev)
    tok_opp, cot_here = lax.optimization_barrier((tok_opp, cotangent))
    cot_following, cot_prev = ring_first(cot_here)
    cot_opp = ring_second(cot_following, cot_prev)
    (tok_full,) = assemble(
        tokens_kernel, [z], [tokens, tok_following, *tok_opp, tok_prev], [(tok_rows, model)]
    )
    enc_k = dot(tok_full, w_ek).astype(bf16)
    enc_v = dot(tok_full, w_ev).astype(bf16)

    attn_flops = 2 * nbr_total * SPAN * width
    sort_flops = 2 * nbr_total * nbr_total * width
    wide = (nbr_total, width)
    narrow = (tok_rows, width)
    (enc_mixed,) = attention_call(
        enc_forward_kernel,
        sources,
        (nbr_all, enc_k, enc_v),
        [wide],
        [wide, wide],
        2 * attn_flops + 2 * sort_flops,
    )
    tok_full, cot_opp, _ = lax.optimization_barrier((tok_full, cot_opp, enc_mixed))
    span_q = dot(tok_full, w_cq).astype(bf16)
    live = jnp.arange(SPANS_SEQ)[None, :] < valid_spans[:, None]
    live_tok = jnp.repeat(live.reshape(-1), SPAN)[:, None]
    (gated,) = assemble(
        cotangent_kernel,
        [z],
        [live_tok.astype(jnp.int32), cotangent, cot_following, *cot_opp, cot_prev],
        [(tok_rows, model)],
    )
    d_cross = dot_nt(gated, w_co).astype(bf16)

    mixed_following, mixed_prev = ring_first(enc_mixed)
    mixed_low, mixed_high = ring_second(mixed_following, mixed_prev)
    kv = nbr_all[:, width:].astype(f32) + dot(enc_mixed, composite[0])
    kv = kv + dot(mixed_following, composite[1]) + dot(mixed_prev, composite[3])
    kv = kv + dot(jnp.concatenate([mixed_low, mixed_high], axis=0), composite[2])
    cross_mixed, d_cq, d_kv = attention_call(
        cross_kernel,
        sources,
        (span_q, kv.astype(bf16), d_cross),
        [narrow, narrow, (nbr_total, 2 * width)],
        [wide] * 4,
        6 * attn_flops + 4 * sort_flops,
    )

    enc_blocks = [dot_nt(d_kv, composite[b]).astype(bf16) for b in range(planes)]
    sends = scatter_sends(enc_blocks)
    sends, d_kv, mixed_here = lax.optimization_barrier((sends, d_kv, cross_mixed))
    enc_left, enc_right = to_right(sends[0]), to_left(sends[1])
    enc_terms = scatter_second(enc_blocks, enc_left, enc_right)
    d_kv_back = spread(d_kv)
    d_wco = lax.psum_scatter(
        dot_tn(gated, mixed_here).astype(bf16), "dp", scatter_dimension=0, tiled=True
    )
    d_wco = d_wco.astype(f32).T

    def plane_blocks(terms):
        return [
            lax.dynamic_slice_in_dim(terms, ((z + b) % planes) * feat_here, feat_here, 1)
            for b in range(planes)
        ]

    out_blocks = plane_blocks(dot(mixed_here, w_co).astype(bf16))
    out_blocks, _ = lax.optimization_barrier((out_blocks, enc_terms[3]))
    out_part = scatter_sum(*scatter_second(out_blocks, *scatter_first(out_blocks)))
    output = (tokens.astype(f32) + jnp.where(live_tok, out_part, 0.0)).astype(bf16)

    d_eq, d_ek, d_ev = attention_call(
        enc_backward_kernel,
        sources,
        (nbr_all, enc_k, enc_v, *enc_terms),
        [wide, narrow, narrow],
        [wide] * 3,
        5 * attn_flops + 3 * sort_flops,
    )
    d_q_back = spread(d_eq)

    tok_blocks = plane_blocks(
        (dot_nt(d_cq, w_cq) + dot_nt(d_ek, w_ek) + dot_nt(d_ev, w_ev)).astype(bf16)
    )
    tok_part = scatter_sum(*scatter_second(tok_blocks, *scatter_first(tok_blocks)))
    d_input = (cotangent.astype(f32) + tok_part).astype(bf16)

    sum_kv = dot_tn(pick, d_kv_back).astype(bf16)
    sum_q = dot_tn(pick, d_q_back).astype(bf16)
    db_terms = (
        dot_nt(sum_kv[:, :width], w_ck) + dot_nt(sum_kv[:, width:], w_cv) + dot_nt(sum_q, w_eq)
    ).astype(bf16)
    db_terms = db_terms.reshape(planes, db_rows, sources, model // sources)
    db_terms = jnp.stack(
        [
            lax.dynamic_index_in_dim(db_terms, (p - z) % planes, 0, keepdims=False)
            for p in range(planes)
        ]
    )
    db_terms = db_terms.transpose(2, 0, 1, 3).reshape(sources * planes, db_rows, model // sources)
    arrived = lax.all_to_all(db_terms, ("dp", "mp"), split_axis=0, concat_axis=0, tiled=True)
    arrived = arrived.reshape(sources, planes, db_here, part, model // sources)
    d_database = (
        jnp.sum(arrived.astype(f32), axis=1)
        .transpose(1, 0, 2, 3)
        .reshape(db_here, nbr_len, model // sources)
    )
    return (output, d_input, d_database, d_wco)


def solution(mesh):
    placed = (
        P("dp", "mp"),
        P("dp", "mp"),
        P("mp", None, None),
        P("dp", None, None),
        P("dp"),
        P(None, "mp"),
        P(None, "mp"),
        P(None, "mp"),
        P("mp", None),
        P(None, "mp"),
        P(None, "mp"),
        P(None, "mp"),
        P("mp", None),
    )
    return jax.shard_map(
        on_device,
        mesh=mesh,
        in_specs=placed,
        out_specs=(P("dp", "mp"), P("dp", "mp"), P("mp", None, "dp"), P("mp", "dp")),
        check_vma=False,
    )
```

```python
import functools
import math

import jax
import jax.numpy as jnp
import numpy as np
from jax import lax
from jax.experimental import pallas as pl
from jax.experimental.pallas import tpu as pltpu
from jax.sharding import PartitionSpec as P

HEAD_DIM = 128
SPAN = 64
SPANS_SEQ = 4
K_NB = 2
INV_SCALE = 1.0 / math.sqrt(HEAD_DIM)
VMEM_LIMIT = 60 * 1024 * 1024


def dot(a, b):
    return jnp.dot(a, b, preferred_element_type=jnp.float32)


def dot_nt(a, b):
    return lax.dot_general(a, b, (((1,), (1,)), ((), ())), preferred_element_type=jnp.float32)


def dot_tn(a, b):
    return lax.dot_general(a, b, (((0,), (0,)), ((), ())), preferred_element_type=jnp.float32)


def to_right(x):
    n = lax.axis_size("mp")
    return lax.ppermute(x, "mp", [(i, (i + 1) % n) for i in range(n)])


def to_left(x):
    n = lax.axis_size("mp")
    return lax.ppermute(x, "mp", [(i, (i - 1) % n) for i in range(n)])


def ring_first(x):
    return to_left(x), to_right(x)


def ring_second(following, prev, axis=0):
    low, _ = jnp.split(prev, 2, axis=axis)
    _, high = jnp.split(following, 2, axis=axis)
    return to_right(low), to_left(high)


def write_block(b, block, refs):
    rightward, leftward, own, next_low, prev_high = refs
    half = block.shape[0] // 2
    if b == 0:
        own[...] = block
    elif b == 1:
        next_low[...] = block[:half]
        rightward[half:] = block[half:]
    elif b == 2:
        rightward[:half] = block[:half]
        leftward[half:] = block[half:]
    else:
        leftward[:half] = block[:half]
        prev_high[...] = block[half:]


def block_shapes(rows, columns):
    return [(rows, columns)] * 3 + [(rows // 2, columns)] * 2


def scatter_second(next_low, prev_high, from_left, from_right):
    half = next_low.shape[0]
    f32 = jnp.float32
    pass_right = next_low.astype(f32) + from_left[:half].astype(f32)
    pass_left = prev_high.astype(f32) + from_right[half:].astype(f32)
    return to_right(pass_right.astype(next_low.dtype)), to_left(pass_left.astype(next_low.dtype))


def scatter_sum(own, from_left, from_right, low, high):
    half = own.shape[0] // 2
    f32 = jnp.float32
    total_low = own[:half].astype(f32) + from_right[:half].astype(f32) + low[...].astype(f32)
    total_high = own[half:].astype(f32) + from_left[half:].astype(f32) + high[...].astype(f32)
    return jnp.concatenate([total_low, total_high], axis=0)


def kernel_call(body, scalars, operands, outs, scratch=(), flops=0, streamed=()):
    vmem = pl.BlockSpec(memory_space=pltpu.VMEM)
    smem = pl.BlockSpec(memory_space=pltpu.SMEM)
    hbm = pl.BlockSpec(memory_space=pltpu.HBM)
    shapes = [o if isinstance(o, jax.ShapeDtypeStruct) else bf16_shape(o) for o in outs]
    streamed = [x if isinstance(x, tuple) else (x, ...) for x in streamed]
    arrays = [*operands, *(x for x, _ in streamed)]
    moved = 2 * (sum(math.prod(x.shape) for x in arrays) + sum(math.prod(o.shape) for o in shapes))
    scratch = list(scratch)
    if streamed:
        places = [place for _, place in streamed]
        body = functools.partial(streaming, body, len(scalars) + len(operands), places)
        scratch += [bf16_scratch(*np.broadcast_to(0, x.shape)[p].shape) for x, p in streamed]
        scratch.append(pltpu.SemaphoreType.DMA((len(streamed),)))
    return pl.pallas_call(
        body,
        out_shape=shapes,
        in_specs=[smem] * len(scalars) + [vmem] * len(operands) + [hbm] * len(streamed),
        out_specs=[vmem] * len(outs),
        scratch_shapes=scratch,
        compiler_params=pltpu.CompilerParams(vmem_limit_bytes=VMEM_LIMIT),
        cost_estimate=pl.CostEstimate(flops=flops, bytes_accessed=moved, transcendentals=0),
    )(*[x.reshape(1) for x in scalars], *arrays)


def streaming(body, first, places, *refs):
    count = len(places)
    held, sems = refs[-1 - count : -1], refs[-1]
    copies = [
        pltpu.make_async_copy(refs[first + n].at[places[n]], held[n], sems.at[n])
        for n in range(count)
    ]
    for copy in copies:
        copy.start()
    waited = set()

    def part(n):
        if n not in waited:
            copies[n].wait()
            waited.add(n)
        return held[n]

    body(part, *refs[:first], *refs[first + count : -1 - count])


def bf16_shape(shape):
    return jax.ShapeDtypeStruct(shape, jnp.bfloat16)


def bf16_scratch(*shape):
    return pltpu.VMEM(shape, jnp.bfloat16)


def held_kernel(weight, own, following, opp_low, opp_high, prev, pick_ref, share_ref, send_ref):
    width = share_ref.shape[1] // 2
    planes = lax.axis_size("mp")
    each = own.shape[0]
    db_rows = pick_ref.shape[1] // planes
    opp = jnp.concatenate([opp_low[...], opp_high[...]], axis=1)
    pieces = [own[...], following[...], opp, prev[...]]
    rows = jnp.concatenate([p.astype(jnp.float32) for p in pieces], axis=0).astype(jnp.bfloat16)
    pick = pick_ref[...]
    for n, place in enumerate((1, 2, 0)):
        projected = dot(rows, weight(n)[...])
        parts = [projected[b * each : (b + 1) * each] for b in range(planes)]
        held = jnp.concatenate([p[:db_rows] for p in parts], axis=0).astype(jnp.bfloat16)
        columns = slice(place * width, (place + 1) * width)
        send_ref[:, columns] = dot(pick, held).astype(jnp.bfloat16)
        if place > 0:
            other = jnp.concatenate([p[db_rows:] for p in parts], axis=0)
            share_ref[:, (place - 1) * width : place * width] = other.astype(jnp.bfloat16)


def place_blocks(z_ref, blocks, out_ref):
    planes = lax.axis_size("mp")
    wide = blocks[0].shape[1]
    half = blocks[2].shape[0]

    def at(b):
        return pl.ds(pl.multiple_of(((z_ref[0] + b) % planes) * wide, wide), wide)

    out_ref[:, at(0)] = blocks[0][...]
    out_ref[:, at(1)] = blocks[1][...]
    out_ref[:half, at(2)] = blocks[2][...]
    out_ref[half:, at(2)] = blocks[3][...]
    out_ref[:, at(3)] = blocks[4][...]


def tokens_kernel(weight, z_ref, *refs):
    k_ref, v_ref, q_ref, whole = refs[5:]
    place_blocks(z_ref, refs[:5], whole)
    k_ref[...] = dot(whole[...], weight(0)[...]).astype(jnp.bfloat16)
    v_ref[...] = dot(whole[...], weight(1)[...]).astype(jnp.bfloat16)
    q_ref[...] = dot(whole[...], weight(2)[...]).astype(jnp.bfloat16)


def cotangent_kernel(weight, z_ref, live_ref, *refs):
    whole, u_ref = refs[5:]
    live = live_ref[...] > 0
    kept = [jnp.where(live[: r.shape[0]], r[...], jnp.zeros_like(r)) for r in refs[:3]]
    kept.append(jnp.where(live[refs[2].shape[0] :], refs[3][...], jnp.zeros_like(refs[3])))
    kept.append(jnp.where(live, refs[4][...], jnp.zeros_like(refs[4])))
    place_blocks(z_ref, kept, whole)
    u_ref[...] = dot_nt(whole[...], weight(0)[...]).astype(jnp.bfloat16)


def plane_products_kernel(count, by_row, weight, z_ref, *refs):
    operands, outs, total = refs[:count], refs[count : count + 5], refs[-1]
    planes = lax.axis_size("mp")
    wide = outs[0].shape[1]
    for n, d_ref in enumerate(operands):
        w_ref = weight(n)
        for b in range(planes):
            at = pl.ds(pl.multiple_of(((z_ref[0] + b) % planes) * wide, wide), wide)
            part = dot_nt(d_ref[...], w_ref[at, :]) if by_row else dot(d_ref[...], w_ref[:, at])
            if n > 0:
                part = part + total[b]
            if n + 1 < count:
                total[b] = part
            else:
                write_block(b, part.astype(jnp.bfloat16), outs)


def plane_products(operands, weights, z, wide, by_row):
    rows, depth = operands[0].shape
    return kernel_call(
        functools.partial(plane_products_kernel, len(operands), by_row),
        [z],
        operands,
        block_shapes(rows, wide),
        [pltpu.VMEM((lax.axis_size("mp"), rows, wide), jnp.float32)],
        2 * len(operands) * rows * math.prod(weights[0].shape),
        weights,
    )


def database_kernel(weight, z_ref, pick_ref, kv_ref, q_ref, out_ref, terms_s):
    planes = lax.axis_size("mp")
    width = q_ref.shape[1]
    pick = pick_ref[...]
    sum_kv = dot(pick, kv_ref[...]).astype(jnp.bfloat16)
    sum_q = dot(pick, q_ref[...]).astype(jnp.bfloat16)
    terms_s[...] = dot_nt(sum_kv[:, :width], weight(0)[...])
    terms_s[...] += dot_nt(sum_kv[:, width:], weight(1)[...])
    terms_s[...] += dot_nt(sum_q, weight(2)[...])
    rows, columns = out_ref.shape[1:]
    for p in range(planes):
        start = pl.multiple_of(((p + planes - z_ref[0]) % planes) * rows, 8)
        block = terms_s[pl.ds(start, rows), :].astype(jnp.bfloat16)
        for j in range(out_ref.shape[0] // planes):
            out_ref[j * planes + p] = block[:, j * columns : (j + 1) * columns]


def order_matrix(rows, sources, inverse):
    per_span = rows // SPANS_SEQ
    chunk = per_span // sources
    block = chunk * SPANS_SEQ
    row = lax.broadcasted_iota(jnp.int32, (rows, 1), 0)
    column = lax.broadcasted_iota(jnp.int32, (rows, rows), 1)
    if inverse:
        place = ((row % block) // chunk) * per_span + (row // block) * chunk + row % chunk
    else:
        place = ((row % per_span) // chunk) * block + (row // per_span) * chunk + row % chunk
    return jnp.where(column == place, 1.0, 0.0).astype(jnp.bfloat16)


def reorder(order, rows):
    return dot(order, rows).astype(jnp.bfloat16)


def softmax_rows(scores):
    top = jnp.max(scores, axis=-1, keepdims=True)
    grown = jnp.exp(scores - top)
    return grown * (1.0 / jnp.sum(grown, axis=-1, keepdims=True))


def tiles(q_rows, k_rows, heads):
    return [
        (
            slice(span * q_rows, (span + 1) * q_rows),
            slice(span * k_rows, (span + 1) * k_rows),
            slice(head * HEAD_DIM, (head + 1) * HEAD_DIM),
        )
        for span in range(SPANS_SEQ)
        for head in range(heads)
    ]


def all_probs(places, q_ref, k_ref):
    scores = [dot_nt(q_ref[q, c], k_ref[k, c]) for q, k, c in places]
    return softmax_rows(jnp.concatenate(scores, axis=0) * INV_SCALE)


def all_backward(places, probs, weights, q_ref, k_ref, v_ref, u_ref, dq_ref, dk_ref, dv_ref):
    d_weights = jnp.concatenate([dot_nt(u_ref[q, c], v_ref[k, c]) for q, k, c in places], axis=0)
    inner = jnp.sum(d_weights * probs, axis=-1, keepdims=True)
    d_scores = (probs * (d_weights - inner)).astype(jnp.bfloat16)
    rows = probs.shape[0] // len(places)
    for n, (q, k, c) in enumerate(places):
        d_s = d_scores[n * rows : (n + 1) * rows]
        dq_ref[q, c] = (dot(d_s, k_ref[k, c]) * INV_SCALE).astype(jnp.bfloat16)
    for n, (q, k, c) in enumerate(places):
        d_s, w = d_scores[n * rows : (n + 1) * rows], weights[n * rows : (n + 1) * rows]
        dk_ref[k, c] = (dot_tn(d_s, q_ref[q, c]) * INV_SCALE).astype(jnp.bfloat16)
        dv_ref[k, c] = dot_tn(w, u_ref[q, c]).astype(jnp.bfloat16)


def mix(places, weights, v_ref, out_ref):
    rows = weights.shape[0] // len(places)
    for n, (q, k, c) in enumerate(places):
        out_ref[q, c] = dot(weights[n * rows : (n + 1) * rows], v_ref[k, c]).astype(jnp.bfloat16)


def enc_forward_kernel(sources, part, k_ref, v_ref, out_ref, q_s, o_s):
    rows, width = out_ref.shape
    q_s[...] = reorder(order_matrix(rows, sources, False), part(0)[...])
    places = tiles(rows // SPANS_SEQ, SPAN, width // HEAD_DIM)
    mix(places, all_probs(places, q_s, k_ref).astype(jnp.bfloat16), v_ref, o_s)
    out_ref[...] = reorder(order_matrix(rows, sources, True), o_s[...])


def keys_kernel(part, own, following, prev, out_ref):
    total = dot(own[...], part(1)[...]) + part(0)[...].astype(jnp.float32)
    total = total + dot(following[...], part(2)[...])
    out_ref[...] = total + dot(prev[...], part(3)[...])


def enc_backward_kernel(sources, part, k_ref, v_ref, *refs):
    terms, (dq_ref, dk_ref, dv_ref, q_s, u_s, dq_s) = refs[:5], refs[5:]
    rows, width = dq_ref.shape
    order = order_matrix(rows, sources, False)
    q_s[...] = reorder(order, part(0)[...])
    u_s[...] = reorder(order, scatter_sum(*terms).astype(jnp.bfloat16))
    places = tiles(rows // SPANS_SEQ, SPAN, width // HEAD_DIM)
    probs = all_probs(places, q_s, k_ref)
    weights = probs.astype(jnp.bfloat16)
    all_backward(places, probs, weights, q_s, k_ref, v_ref, u_s, dq_s, dk_ref, dv_ref)
    dq_ref[...] = reorder(order_matrix(rows, sources, True), dq_s[...])


def cross_kernel(sources, part, q_ref, part_ref, low_ref, high_ref, u_ref, *refs):
    o_ref, dq_ref, dkv_ref = refs[:3]
    blocks, (k_s, v_s, dk_s, dv_s) = refs[3:8], refs[8:]
    rows, both = part_ref.shape
    width = both // 2
    mixed = jnp.concatenate([low_ref[...], high_ref[...]], axis=0)
    kv = (part_ref[...] + dot(mixed, part(0)[...])).astype(jnp.bfloat16)
    order = order_matrix(rows, sources, False)
    k_s[...] = reorder(order, kv[:, :width])
    v_s[...] = reorder(order, kv[:, width:])
    places = tiles(SPAN, rows // SPANS_SEQ, width // HEAD_DIM)
    probs = all_probs(places, q_ref, k_s)
    weights = probs.astype(jnp.bfloat16)
    mix(places, weights, v_s, o_ref)
    all_backward(places, probs, weights, q_ref, k_s, v_s, u_ref, dq_ref, dk_s, dv_s)
    back = order_matrix(rows, sources, True)
    dkv_ref[:, :width] = reorder(back, dk_s[...])
    dkv_ref[:, width:] = reorder(back, dv_s[...])
    for n, b in enumerate((2, 1, 3, 0)):
        write_block(b, dot_nt(dkv_ref[...], part(n)[...]).astype(jnp.bfloat16), blocks)


def on_device(
    tokens,
    cotangent,
    database,
    neighbour_ids,
    valid_spans,
    w_cq,
    w_ck,
    w_cv,
    w_co,
    w_eq,
    w_ek,
    w_ev,
    w_eo,
):
    bf16, f32 = jnp.bfloat16, jnp.float32
    width = w_cq.shape[1]
    heads = width // HEAD_DIM
    tok_rows, feat_here = tokens.shape
    model = w_cq.shape[0]
    db_here, nbr_len, _ = database.shape
    planes = lax.axis_size("mp")
    sources = lax.axis_size("dp")
    z = lax.axis_index("mp")
    i = lax.axis_index("dp")
    nbr_count = neighbour_ids.size
    part = nbr_len // sources
    db_rows = db_here * part
    eo_rows = width // sources
    nbr_total = nbr_count * nbr_len

    def spread(x):
        return lax.all_to_all(x, "dp", split_axis=0, concat_axis=0, tiled=True)

    db_own = lax.dynamic_slice_in_dim(database, i * part, part, 1).reshape(db_rows, model)
    eo_own = lax.dynamic_slice_in_dim(w_eo, i * eo_rows, eo_rows, 0)
    rows_own = jnp.concatenate([db_own, eo_own], axis=0)
    rows_following, rows_prev = ring_first(rows_own)
    rows_following, rows_prev, asked_here, cot_here = lax.optimization_barrier(
        (rows_following, rows_prev, neighbour_ids.reshape(1, -1), cotangent)
    )
    ids = spread(jnp.broadcast_to(asked_here, (sources, nbr_count))).reshape(-1)
    tok_following, tok_prev = ring_first(tokens)
    rows_low, rows_high = ring_second(rows_following, rows_prev, 1)
    cot_following, cot_prev = ring_first(cot_here)
    rows_low, rows_high, ids, tok_following, tok_prev = lax.optimization_barrier(
        (rows_low, rows_high, ids, tok_following, tok_prev)
    )

    held_rows = planes * db_rows
    asked = jnp.repeat(ids, part)
    asked_tok = jnp.arange(nbr_total) % part

    def picks(shape, held_dim):
        held = lax.broadcasted_iota(jnp.int32, shape, held_dim)
        held_id = ((z + held // db_rows) % planes) * db_here + (held % db_rows) // part
        wanted, wanted_tok = (jnp.expand_dims(x, held_dim) for x in (asked, asked_tok))
        return ((wanted == held_id) & (wanted_tok == held % part)).astype(bf16)

    pick = picks((1, held_rows), 1)
    pick_back = picks((held_rows, 1), 0)
    share, nbr_send = kernel_call(
        held_kernel,
        [],
        [rows_own, rows_following, rows_low, rows_high, rows_prev, pick],
        [(planes * eo_rows, 2 * width), (nbr_total, 3 * width)],
        flops=6 * planes * rows_own.shape[0] * model * width,
        streamed=[w_ck, w_cv, w_eq],
    )
    composite = lax.all_gather(
        share.reshape(planes, eo_rows, 2 * width), "dp", axis=1, tiled=True
    )
    nbr_all = spread(nbr_send)

    tok_opp = ring_second(tok_following, tok_prev)
    cot_opp = ring_second(cot_following, cot_prev)
    whole = (tok_rows, model)
    wide = (nbr_total, width)
    narrow = (tok_rows, width)
    enc_k, enc_v, span_q = kernel_call(
        tokens_kernel,
        [z],
        [tokens, tok_following, *tok_opp, tok_prev],
        [narrow, narrow, narrow],
        [bf16_scratch(*whole)],
        6 * tok_rows * model * width,
        [w_ek, w_ev, w_cq],
    )

    live = jnp.arange(SPANS_SEQ)[None, :] < valid_spans[:, None]
    live_tok = jnp.repeat(live.reshape(-1), SPAN)[:, None]
    nbr_all, cot_opp = lax.optimization_barrier((nbr_all, cot_opp))
    gated, d_cross = kernel_call(
        cotangent_kernel,
        [z],
        [
            live_tok.astype(jnp.int32),
            cotangent,
            cot_following,
            *cot_opp,
            cot_prev,
        ],
        [whole, narrow],
        flops=2 * tok_rows * model * width,
        streamed=[w_co],
    )


    attn_flops = 2 * nbr_total * SPAN * width
    sort_flops = 2 * nbr_total * nbr_total * width
    (enc_mixed,) = kernel_call(
        functools.partial(enc_forward_kernel, sources),
        [],
        [enc_k, enc_v],
        [wide],
        [bf16_scratch(*wide)] * 2,
        2 * attn_flops + 2 * sort_flops,
        [(nbr_all, (slice(None), slice(0, width)))],
    )
    mixed_following, mixed_prev = ring_first(enc_mixed)

    mixed_following, mixed_prev, d_cross = lax.optimization_barrier(
        (mixed_following, mixed_prev, d_cross)
    )
    mixed_low, mixed_high = ring_second(mixed_following, mixed_prev)
    (kv_part,) = kernel_call(
        keys_kernel,
        [],
        [enc_mixed, mixed_following, mixed_prev],
        [jax.ShapeDtypeStruct((nbr_total, 2 * width), f32)],
        flops=12 * nbr_total * width * width,
        streamed=[
            (nbr_all, (slice(None), slice(width, 3 * width))),
            *[(composite, b) for b in (0, 1, 3)],
        ],
    )
    cross_mixed, d_cq, d_kv, *enc_blocks = kernel_call(
        functools.partial(cross_kernel, sources),
        [],
        [span_q, kv_part, mixed_low, mixed_high, d_cross],
        [narrow, narrow, (nbr_total, 2 * width)] + block_shapes(*wide),
        [bf16_scratch(*wide)] * 4,
        6 * attn_flops + 4 * sort_flops + 20 * nbr_total * width * width,
        [(composite, b) for b in (2, 1, 3, 0)],
    )

    rightward, leftward, enc_own, enc_next, enc_prev = enc_blocks
    enc_left, enc_right = to_right(rightward), to_left(leftward)
    enc_last = scatter_second(enc_next, enc_prev, enc_left, enc_right)
    d_kv_back = spread(d_kv)
    mixed_here, _ = lax.optimization_barrier((cross_mixed, enc_left))
    out_right, out_left, *out_rest = plane_products([mixed_here], [w_co], z, feat_here, False)
    d_wco = lax.psum_scatter(
        dot_tn(gated, cross_mixed).astype(bf16), "dp", scatter_dimension=0, tiled=True
    )
    d_wco = d_wco.astype(f32).T

    d_eq, d_ek, d_ev = kernel_call(
        functools.partial(enc_backward_kernel, sources),
        [],
        [enc_k, enc_v, enc_own, enc_left, enc_right, *enc_last],
        [wide, narrow, narrow],
        [bf16_scratch(*wide)] * 3,
        5 * attn_flops + 3 * sort_flops,
        [(nbr_all, (slice(None), slice(0, width)))],
    )
    d_q_back = spread(d_eq)
    d_kv_back, d_q_back = lax.optimization_barrier((d_kv_back, d_q_back))

    out_right, out_left, _ = lax.optimization_barrier((out_right, out_left, enc_last[0]))
    out_first = to_right(out_right), to_left(out_left)
    out_last = scatter_second(*out_rest[1:], *out_first)
    out_part = scatter_sum(out_rest[0], *out_first, *out_last)
    output = (tokens.astype(f32) + jnp.where(live_tok, out_part, 0.0)).astype(bf16)

    tok_right, tok_left, *tok_rest = plane_products(
        [d_cq, d_ek, d_ev], [w_cq, w_ek, w_ev], z, feat_here, True
    )
    (db_terms,) = kernel_call(
        database_kernel,
        [z],
        [pick_back, d_kv_back, d_q_back],
        [(sources * planes, db_rows, model // sources)],
        [pltpu.VMEM((held_rows, model), f32)],
        6 * held_rows * width * (nbr_total + model),
        [w_ck, w_cv, w_eq],
    )
    tok_right, tok_left, db_terms = lax.optimization_barrier((tok_right, tok_left, db_terms))
    tok_first = to_right(tok_right), to_left(tok_left)
    tok_last = scatter_second(*tok_rest[1:], *tok_first)
    tok_part = scatter_sum(tok_rest[0], *tok_first, *tok_last)
    d_input = (cotangent.astype(f32) + tok_part).astype(bf16)

    arrived = lax.all_to_all(db_terms, ("dp", "mp"), split_axis=0, concat_axis=0, tiled=True)
    arrived = arrived.reshape(sources, planes, db_here, part, model // sources)
    d_database = (
        jnp.sum(arrived.astype(f32), axis=1)
        .transpose(1, 0, 2, 3)
        .reshape(db_here, nbr_len, model // sources)
    )
    return (output, d_input, d_database, d_wco)


def solution(mesh):
    placed = (
        P("dp", "mp"),
        P("dp", "mp"),
        P("mp", None, None),
        P("dp", None, None),
        P("dp"),
        P(None, "mp"),
        P(None, "mp"),
        P(None, "mp"),
        P("mp", None),
        P(None, "mp"),
        P(None, "mp"),
        P(None, "mp"),
        P("mp", None),
    )
    return jax.shard_map(
        on_device,
        mesh=mesh,
        in_specs=placed,
        out_specs=(P("dp", "mp"), P("dp", "mp"), P("mp", None, "dp"), P("mp", "dp")),
        check_vma=False,
    )
```

```python
import functools
import math

import jax
import jax.numpy as jnp
import numpy as np
from jax import lax
from jax.experimental import pallas as pl
from jax.experimental.pallas import tpu as pltpu
from jax.sharding import PartitionSpec as P

HEAD_DIM = 128
SPAN = 64
SPANS_SEQ = 4
K_NB = 2
INV_SCALE = 1.0 / math.sqrt(HEAD_DIM)
VMEM_LIMIT = 60 * 1024 * 1024


def dot(a, b):
    return jnp.dot(a, b, preferred_element_type=jnp.float32)


def dot_nt(a, b):
    return lax.dot_general(a, b, (((1,), (1,)), ((), ())), preferred_element_type=jnp.float32)


def dot_tn(a, b):
    return lax.dot_general(a, b, (((0,), (0,)), ((), ())), preferred_element_type=jnp.float32)


def to_right(x):
    n = lax.axis_size("mp")
    return lax.ppermute(x, "mp", [(i, (i + 1) % n) for i in range(n)])


def to_left(x):
    n = lax.axis_size("mp")
    return lax.ppermute(x, "mp", [(i, (i - 1) % n) for i in range(n)])


def ring_first(x):
    return to_left(x), to_right(x)


def ring_second(following, prev, axis=0):
    low, _ = jnp.split(prev, 2, axis=axis)
    _, high = jnp.split(following, 2, axis=axis)
    return to_right(low), to_left(high)


def write_block(b, block, refs):
    rightward, leftward, own, next_low, prev_high = refs
    half = block.shape[0] // 2
    if b == 0:
        own[...] = block
    elif b == 1:
        next_low[...] = block[:half]
        rightward[half:] = block[half:]
    elif b == 2:
        rightward[:half] = block[:half]
        leftward[half:] = block[half:]
    else:
        leftward[:half] = block[:half]
        prev_high[...] = block[half:]


def block_shapes(rows, columns):
    return [(rows, columns)] * 3 + [(rows // 2, columns)] * 2


def scatter_second(next_low, prev_high, from_left, from_right):
    half = next_low.shape[0]
    f32 = jnp.float32
    pass_right = next_low.astype(f32) + from_left[:half].astype(f32)
    pass_left = prev_high.astype(f32) + from_right[half:].astype(f32)
    return to_right(pass_right.astype(next_low.dtype)), to_left(pass_left.astype(next_low.dtype))


def scatter_sum(own, from_left, from_right, low, high):
    half = own.shape[0] // 2
    f32 = jnp.float32
    total_low = own[:half].astype(f32) + from_right[:half].astype(f32) + low[...].astype(f32)
    total_high = own[half:].astype(f32) + from_left[half:].astype(f32) + high[...].astype(f32)
    return jnp.concatenate([total_low, total_high], axis=0)


def kernel_call(body, scalars, operands, outs, scratch=(), flops=0, streamed=()):
    vmem = pl.BlockSpec(memory_space=pltpu.VMEM)
    smem = pl.BlockSpec(memory_space=pltpu.SMEM)
    hbm = pl.BlockSpec(memory_space=pltpu.HBM)
    shapes = [o if isinstance(o, jax.ShapeDtypeStruct) else bf16_shape(o) for o in outs]
    streamed = [x if isinstance(x, tuple) else (x, ...) for x in streamed]
    arrays = [*operands, *(x for x, _ in streamed)]
    moved = 2 * (sum(math.prod(x.shape) for x in arrays) + sum(math.prod(o.shape) for o in shapes))
    scratch = list(scratch)
    if streamed:
        places = [place for _, place in streamed]
        body = functools.partial(streaming, body, len(scalars) + len(operands), places)
        scratch += [bf16_scratch(*np.broadcast_to(0, x.shape)[p].shape) for x, p in streamed]
        scratch.append(pltpu.SemaphoreType.DMA((len(streamed),)))
    return pl.pallas_call(
        body,
        out_shape=shapes,
        in_specs=[smem] * len(scalars) + [vmem] * len(operands) + [hbm] * len(streamed),
        out_specs=[vmem] * len(outs),
        scratch_shapes=scratch,
        compiler_params=pltpu.CompilerParams(vmem_limit_bytes=VMEM_LIMIT),
        cost_estimate=pl.CostEstimate(flops=flops, bytes_accessed=moved, transcendentals=0),
    )(*[x.reshape(1) for x in scalars], *arrays)


def streaming(body, first, places, *refs):
    count = len(places)
    held, sems = refs[-1 - count : -1], refs[-1]
    copies = [
        pltpu.make_async_copy(refs[first + n].at[places[n]], held[n], sems.at[n])
        for n in range(count)
    ]
    for copy in copies:
        copy.start()
    waited = set()

    def part(n):
        if n not in waited:
            copies[n].wait()
            waited.add(n)
        return held[n]

    body(part, *refs[:first], *refs[first + count : -1 - count])


def bf16_shape(shape):
    return jax.ShapeDtypeStruct(shape, jnp.bfloat16)


def bf16_scratch(*shape):
    return pltpu.VMEM(shape, jnp.bfloat16)


def held_kernel(weight, own, following, opp_low, opp_high, prev, pick_ref, share_ref, send_ref):
    width = share_ref.shape[1] // 2
    planes = lax.axis_size("mp")
    each = own.shape[0]
    db_rows = pick_ref.shape[1] // planes
    opp = jnp.concatenate([opp_low[...], opp_high[...]], axis=1)
    pieces = [own[...], following[...], opp, prev[...]]
    rows = jnp.concatenate([p.astype(jnp.float32) for p in pieces], axis=0).astype(jnp.bfloat16)
    pick = pick_ref[...]
    for n, place in enumerate((1, 2, 0)):
        projected = dot(rows, weight(n)[...])
        parts = [projected[b * each : (b + 1) * each] for b in range(planes)]
        held = jnp.concatenate([p[:db_rows] for p in parts], axis=0).astype(jnp.bfloat16)
        columns = slice(place * width, (place + 1) * width)
        send_ref[:, columns] = dot(pick, held).astype(jnp.bfloat16)
        if place > 0:
            other = jnp.concatenate([p[db_rows:] for p in parts], axis=0)
            share_ref[:, (place - 1) * width : place * width] = other.astype(jnp.bfloat16)


def place_blocks(z_ref, blocks, out_ref):
    planes = lax.axis_size("mp")
    wide = blocks[0].shape[1]
    half = blocks[2].shape[0]

    def at(b):
        return pl.ds(pl.multiple_of(((z_ref[0] + b) % planes) * wide, wide), wide)

    out_ref[:, at(0)] = blocks[0][...]
    out_ref[:, at(1)] = blocks[1][...]
    out_ref[:half, at(2)] = blocks[2][...]
    out_ref[half:, at(2)] = blocks[3][...]
    out_ref[:, at(3)] = blocks[4][...]


def tokens_kernel(weight, z_ref, *refs):
    k_ref, v_ref, whole = refs[5:]
    place_blocks(z_ref, refs[:5], whole)
    k_ref[...] = dot(whole[...], weight(0)[...]).astype(jnp.bfloat16)
    v_ref[...] = dot(whole[...], weight(1)[...]).astype(jnp.bfloat16)


def cotangent_kernel(weight, z_ref, live_ref, *refs):
    whole, u_ref, q_ref, tok_whole = refs[10:]
    live = live_ref[...] > 0
    kept = [jnp.where(live[: r.shape[0]], r[...], jnp.zeros_like(r)) for r in refs[:3]]
    kept.append(jnp.where(live[refs[2].shape[0] :], refs[3][...], jnp.zeros_like(refs[3])))
    kept.append(jnp.where(live, refs[4][...], jnp.zeros_like(refs[4])))
    place_blocks(z_ref, kept, whole)
    u_ref[...] = dot_nt(whole[...], weight(0)[...]).astype(jnp.bfloat16)
    place_blocks(z_ref, refs[5:10], tok_whole)
    q_ref[...] = dot(tok_whole[...], weight(1)[...]).astype(jnp.bfloat16)


def plane_products_kernel(count, by_row, weight, z_ref, *refs):
    operands, outs, total = refs[:count], refs[count : count + 5], refs[-1]
    planes = lax.axis_size("mp")
    wide = outs[0].shape[1]
    for n, d_ref in enumerate(operands):
        w_ref = weight(n)
        for b in range(planes):
            at = pl.ds(pl.multiple_of(((z_ref[0] + b) % planes) * wide, wide), wide)
            part = dot_nt(d_ref[...], w_ref[at, :]) if by_row else dot(d_ref[...], w_ref[:, at])
            if n > 0:
                part = part + total[b]
            if n + 1 < count:
                total[b] = part
            else:
                write_block(b, part.astype(jnp.bfloat16), outs)


def plane_products(operands, weights, z, wide, by_row):
    rows, depth = operands[0].shape
    return kernel_call(
        functools.partial(plane_products_kernel, len(operands), by_row),
        [z],
        operands,
        block_shapes(rows, wide),
        [pltpu.VMEM((lax.axis_size("mp"), rows, wide), jnp.float32)],
        2 * len(operands) * rows * math.prod(weights[0].shape),
        weights,
    )


def database_kernel(weight, z_ref, pick_ref, kv_ref, q_ref, out_ref, terms_s):
    planes = lax.axis_size("mp")
    width = q_ref.shape[1]
    pick = pick_ref[...]
    sum_kv = dot(pick, kv_ref[...]).astype(jnp.bfloat16)
    sum_q = dot(pick, q_ref[...]).astype(jnp.bfloat16)
    terms_s[...] = dot_nt(sum_kv[:, :width], weight(0)[...])
    terms_s[...] += dot_nt(sum_kv[:, width:], weight(1)[...])
    terms_s[...] += dot_nt(sum_q, weight(2)[...])
    rows, columns = out_ref.shape[1:]
    for p in range(planes):
        start = pl.multiple_of(((p + planes - z_ref[0]) % planes) * rows, 8)
        block = terms_s[pl.ds(start, rows), :].astype(jnp.bfloat16)
        for j in range(out_ref.shape[0] // planes):
            out_ref[j * planes + p] = block[:, j * columns : (j + 1) * columns]


def order_matrix(rows, sources, inverse):
    per_span = rows // SPANS_SEQ
    chunk = per_span // sources
    block = chunk * SPANS_SEQ
    row = lax.broadcasted_iota(jnp.int32, (rows, 1), 0)
    column = lax.broadcasted_iota(jnp.int32, (rows, rows), 1)
    if inverse:
        place = ((row % block) // chunk) * per_span + (row // block) * chunk + row % chunk
    else:
        place = ((row % per_span) // chunk) * block + (row // per_span) * chunk + row % chunk
    return jnp.where(column == place, 1.0, 0.0).astype(jnp.bfloat16)


def reorder(order, rows):
    return dot(order, rows).astype(jnp.bfloat16)


def softmax_rows(scores):
    top = jnp.max(scores, axis=-1, keepdims=True)
    grown = jnp.exp(scores - top)
    return grown * (1.0 / jnp.sum(grown, axis=-1, keepdims=True))


def tiles(q_rows, k_rows, heads):
    return [
        (
            slice(span * q_rows, (span + 1) * q_rows),
            slice(span * k_rows, (span + 1) * k_rows),
            slice(head * HEAD_DIM, (head + 1) * HEAD_DIM),
        )
        for span in range(SPANS_SEQ)
        for head in range(heads)
    ]


def all_probs(places, q_ref, k_ref):
    scores = [dot_nt(q_ref[q, c], k_ref[k, c]) for q, k, c in places]
    return softmax_rows(jnp.concatenate(scores, axis=0) * INV_SCALE)


def all_backward(places, probs, weights, q_ref, k_ref, v_ref, u_ref, dq_ref, dk_ref, dv_ref):
    d_weights = jnp.concatenate([dot_nt(u_ref[q, c], v_ref[k, c]) for q, k, c in places], axis=0)
    inner = jnp.sum(d_weights * probs, axis=-1, keepdims=True)
    d_scores = (probs * (d_weights - inner)).astype(jnp.bfloat16)
    rows = probs.shape[0] // len(places)
    for n, (q, k, c) in enumerate(places):
        d_s = d_scores[n * rows : (n + 1) * rows]
        dq_ref[q, c] = (dot(d_s, k_ref[k, c]) * INV_SCALE).astype(jnp.bfloat16)
    for n, (q, k, c) in enumerate(places):
        d_s, w = d_scores[n * rows : (n + 1) * rows], weights[n * rows : (n + 1) * rows]
        dk_ref[k, c] = (dot_tn(d_s, q_ref[q, c]) * INV_SCALE).astype(jnp.bfloat16)
        dv_ref[k, c] = dot_tn(w, u_ref[q, c]).astype(jnp.bfloat16)


def mix(places, weights, v_ref, out_ref):
    rows = weights.shape[0] // len(places)
    for n, (q, k, c) in enumerate(places):
        out_ref[q, c] = dot(weights[n * rows : (n + 1) * rows], v_ref[k, c]).astype(jnp.bfloat16)


def enc_forward_kernel(sources, part, k_ref, v_ref, out_ref, q_s, o_s):
    rows, width = out_ref.shape
    q_s[...] = reorder(order_matrix(rows, sources, False), part(0)[...])
    places = tiles(rows // SPANS_SEQ, SPAN, width // HEAD_DIM)
    mix(places, all_probs(places, q_s, k_ref).astype(jnp.bfloat16), v_ref, o_s)
    out_ref[...] = reorder(order_matrix(rows, sources, True), o_s[...])


def keys_kernel(part, own, following, prev, out_ref):
    total = dot(own[...], part(1)[...]) + part(0)[...].astype(jnp.float32)
    total = total + dot(following[...], part(2)[...])
    out_ref[...] = total + dot(prev[...], part(3)[...])


def enc_backward_kernel(sources, part, k_ref, v_ref, *refs):
    terms, (dq_ref, dk_ref, dv_ref, q_s, u_s, dq_s) = refs[:5], refs[5:]
    rows, width = dq_ref.shape
    order = order_matrix(rows, sources, False)
    q_s[...] = reorder(order, part(0)[...])
    u_s[...] = reorder(order, scatter_sum(*terms).astype(jnp.bfloat16))
    places = tiles(rows // SPANS_SEQ, SPAN, width // HEAD_DIM)
    probs = all_probs(places, q_s, k_ref)
    weights = probs.astype(jnp.bfloat16)
    all_backward(places, probs, weights, q_s, k_ref, v_ref, u_s, dq_s, dk_ref, dv_ref)
    dq_ref[...] = reorder(order_matrix(rows, sources, True), dq_s[...])


def cross_kernel(sources, part, q_ref, part_ref, low_ref, high_ref, u_ref, *refs):
    o_ref, dq_ref, dkv_ref = refs[:3]
    blocks, (k_s, v_s, dk_s, dv_s) = refs[3:8], refs[8:]
    rows, both = part_ref.shape
    width = both // 2
    mixed = jnp.concatenate([low_ref[...], high_ref[...]], axis=0)
    kv = (part_ref[...] + dot(mixed, part(0)[...])).astype(jnp.bfloat16)
    order = order_matrix(rows, sources, False)
    k_s[...] = reorder(order, kv[:, :width])
    v_s[...] = reorder(order, kv[:, width:])
    places = tiles(SPAN, rows // SPANS_SEQ, width // HEAD_DIM)
    probs = all_probs(places, q_ref, k_s)
    weights = probs.astype(jnp.bfloat16)
    mix(places, weights, v_s, o_ref)
    all_backward(places, probs, weights, q_ref, k_s, v_s, u_ref, dq_ref, dk_s, dv_s)
    back = order_matrix(rows, sources, True)
    dkv_ref[:, :width] = reorder(back, dk_s[...])
    dkv_ref[:, width:] = reorder(back, dv_s[...])
    for n, b in enumerate((2, 1, 3, 0)):
        write_block(b, dot_nt(dkv_ref[...], part(n)[...]).astype(jnp.bfloat16), blocks)


def on_device(
    tokens,
    cotangent,
    database,
    neighbour_ids,
    valid_spans,
    w_cq,
    w_ck,
    w_cv,
    w_co,
    w_eq,
    w_ek,
    w_ev,
    w_eo,
):
    bf16, f32 = jnp.bfloat16, jnp.float32
    width = w_cq.shape[1]
    heads = width // HEAD_DIM
    tok_rows, feat_here = tokens.shape
    model = w_cq.shape[0]
    db_here, nbr_len, _ = database.shape
    planes = lax.axis_size("mp")
    sources = lax.axis_size("dp")
    z = lax.axis_index("mp")
    i = lax.axis_index("dp")
    nbr_count = neighbour_ids.size
    part = nbr_len // sources
    db_rows = db_here * part
    eo_rows = width // sources
    nbr_total = nbr_count * nbr_len

    def spread(x):
        return lax.all_to_all(x, "dp", split_axis=0, concat_axis=0, tiled=True)

    db_own = lax.dynamic_slice_in_dim(database, i * part, part, 1).reshape(db_rows, model)
    eo_own = lax.dynamic_slice_in_dim(w_eo, i * eo_rows, eo_rows, 0)
    rows_own = jnp.concatenate([db_own, eo_own], axis=0)
    rows_following, rows_prev = ring_first(rows_own)
    rows_following, rows_prev, asked_here, cot_here = lax.optimization_barrier(
        (rows_following, rows_prev, neighbour_ids.reshape(1, -1), cotangent)
    )
    ids = spread(jnp.broadcast_to(asked_here, (sources, nbr_count))).reshape(-1)
    tok_following, tok_prev = ring_first(tokens)
    rows_low, rows_high = ring_second(rows_following, rows_prev, 1)
    cot_following, cot_prev = ring_first(cot_here)
    rows_low, rows_high, ids, tok_following, tok_prev = lax.optimization_barrier(
        (rows_low, rows_high, ids, tok_following, tok_prev)
    )

    held_rows = planes * db_rows
    asked = jnp.repeat(ids, part)
    asked_tok = jnp.arange(nbr_total) % part

    def picks(shape, held_dim):
        held = lax.broadcasted_iota(jnp.int32, shape, held_dim)
        held_id = ((z + held // db_rows) % planes) * db_here + (held % db_rows) // part
        wanted, wanted_tok = (jnp.expand_dims(x, held_dim) for x in (asked, asked_tok))
        return ((wanted == held_id) & (wanted_tok == held % part)).astype(bf16)

    pick = picks((1, held_rows), 1)
    pick_back = picks((held_rows, 1), 0)
    share, nbr_send = kernel_call(
        held_kernel,
        [],
        [rows_own, rows_following, rows_low, rows_high, rows_prev, pick],
        [(planes * eo_rows, 2 * width), (nbr_total, 3 * width)],
        flops=6 * planes * rows_own.shape[0] * model * width,
        streamed=[w_ck, w_cv, w_eq],
    )
    composite = lax.all_gather(
        share.reshape(planes, eo_rows, 2 * width), "dp", axis=1, tiled=True
    )
    nbr_all = spread(nbr_send)

    tok_opp = ring_second(tok_following, tok_prev)
    cot_opp = ring_second(cot_following, cot_prev)
    whole = (tok_rows, model)
    wide = (nbr_total, width)
    narrow = (tok_rows, width)
    enc_k, enc_v = kernel_call(
        tokens_kernel,
        [z],
        [tokens, tok_following, *tok_opp, tok_prev],
        [narrow, narrow],
        [bf16_scratch(*whole)],
        4 * tok_rows * model * width,
        [w_ek, w_ev],
    )

    live = jnp.arange(SPANS_SEQ)[None, :] < valid_spans[:, None]
    live_tok = jnp.repeat(live.reshape(-1), SPAN)[:, None]
    nbr_all, cot_opp = lax.optimization_barrier((nbr_all, cot_opp))
    gated, d_cross, span_q = kernel_call(
        cotangent_kernel,
        [z],
        [
            live_tok.astype(jnp.int32),
            cotangent,
            cot_following,
            *cot_opp,
            cot_prev,
            tokens,
            tok_following,
            *tok_opp,
            tok_prev,
        ],
        [whole, narrow, narrow],
        [bf16_scratch(*whole)],
        4 * tok_rows * model * width,
        [w_co, w_cq],
    )


    attn_flops = 2 * nbr_total * SPAN * width
    sort_flops = 2 * nbr_total * nbr_total * width
    (enc_mixed,) = kernel_call(
        functools.partial(enc_forward_kernel, sources),
        [],
        [enc_k, enc_v],
        [wide],
        [bf16_scratch(*wide)] * 2,
        2 * attn_flops + 2 * sort_flops,
        [(nbr_all, (slice(None), slice(0, width)))],
    )
    mixed_following, mixed_prev = ring_first(enc_mixed)

    mixed_following, mixed_prev, d_cross = lax.optimization_barrier(
        (mixed_following, mixed_prev, d_cross)
    )
    mixed_low, mixed_high = ring_second(mixed_following, mixed_prev)
    (kv_part,) = kernel_call(
        keys_kernel,
        [],
        [enc_mixed, mixed_following, mixed_prev],
        [jax.ShapeDtypeStruct((nbr_total, 2 * width), f32)],
        flops=12 * nbr_total * width * width,
        streamed=[
            (nbr_all, (slice(None), slice(width, 3 * width))),
            *[(composite, b) for b in (0, 1, 3)],
        ],
    )
    cross_mixed, d_cq, d_kv, *enc_blocks = kernel_call(
        functools.partial(cross_kernel, sources),
        [],
        [span_q, kv_part, mixed_low, mixed_high, d_cross],
        [narrow, narrow, (nbr_total, 2 * width)] + block_shapes(*wide),
        [bf16_scratch(*wide)] * 4,
        6 * attn_flops + 4 * sort_flops + 20 * nbr_total * width * width,
        [(composite, b) for b in (2, 1, 3, 0)],
    )

    rightward, leftward, enc_own, enc_next, enc_prev = enc_blocks
    enc_left, enc_right = to_right(rightward), to_left(leftward)
    enc_last = scatter_second(enc_next, enc_prev, enc_left, enc_right)
    d_kv_back = spread(d_kv)
    mixed_here, _ = lax.optimization_barrier((cross_mixed, enc_left))
    out_right, out_left, *out_rest = plane_products([mixed_here], [w_co], z, feat_here, False)
    d_wco = lax.psum_scatter(
        dot_tn(gated, cross_mixed).astype(bf16), "dp", scatter_dimension=0, tiled=True
    )
    d_wco = d_wco.astype(f32).T

    d_eq, d_ek, d_ev = kernel_call(
        functools.partial(enc_backward_kernel, sources),
        [],
        [enc_k, enc_v, enc_own, enc_left, enc_right, *enc_last],
        [wide, narrow, narrow],
        [bf16_scratch(*wide)] * 3,
        5 * attn_flops + 3 * sort_flops,
        [(nbr_all, (slice(None), slice(0, width)))],
    )
    d_q_back = spread(d_eq)
    d_kv_back, d_q_back = lax.optimization_barrier((d_kv_back, d_q_back))

    out_right, out_left, _ = lax.optimization_barrier((out_right, out_left, enc_last[0]))
    out_first = to_right(out_right), to_left(out_left)
    out_last = scatter_second(*out_rest[1:], *out_first)
    out_part = scatter_sum(out_rest[0], *out_first, *out_last)
    output = (tokens.astype(f32) + jnp.where(live_tok, out_part, 0.0)).astype(bf16)

    tok_right, tok_left, *tok_rest = plane_products(
        [d_cq, d_ek, d_ev], [w_cq, w_ek, w_ev], z, feat_here, True
    )
    (db_terms,) = kernel_call(
        database_kernel,
        [z],
        [pick_back, d_kv_back, d_q_back],
        [(sources * planes, db_rows, model // sources)],
        [pltpu.VMEM((held_rows, model), f32)],
        6 * held_rows * width * (nbr_total + model),
        [w_ck, w_cv, w_eq],
    )
    tok_right, tok_left, db_terms = lax.optimization_barrier((tok_right, tok_left, db_terms))
    tok_first = to_right(tok_right), to_left(tok_left)
    tok_last = scatter_second(*tok_rest[1:], *tok_first)
    tok_part = scatter_sum(tok_rest[0], *tok_first, *tok_last)
    d_input = (cotangent.astype(f32) + tok_part).astype(bf16)

    arrived = lax.all_to_all(db_terms, ("dp", "mp"), split_axis=0, concat_axis=0, tiled=True)
    arrived = arrived.reshape(sources, planes, db_here, part, model // sources)
    d_database = (
        jnp.sum(arrived.astype(f32), axis=1)
        .transpose(1, 0, 2, 3)
        .reshape(db_here, nbr_len, model // sources)
    )
    return (output, d_input, d_database, d_wco)


def solution(mesh):
    placed = (
        P("dp", "mp"),
        P("dp", "mp"),
        P("mp", None, None),
        P("dp", None, None),
        P("dp"),
        P(None, "mp"),
        P(None, "mp"),
        P(None, "mp"),
        P("mp", None),
        P(None, "mp"),
        P(None, "mp"),
        P(None, "mp"),
        P("mp", None),
    )
    return jax.shard_map(
        on_device,
        mesh=mesh,
        in_specs=placed,
        out_specs=(P("dp", "mp"), P("dp", "mp"), P("mp", None, "dp"), P("mp", "dp")),
        check_vma=False,
    )
```
